1024 devices in a mesh: fsdp: 64 (over x, z), dp: 16 (over y, core).
Axes of the slice: x: 8, y: 8, z: 8, core: 2. Of those that a mesh axis runs over, the one named last changes fastest.
Arguments:
- grad_out: bfloat16 [4096, 8192], P('dp', 'fsdp'), may hold values from -6 to 6
- hidden: bfloat16 [4096, 28672], P('dp', 'fsdp'), may hold values from -6 to 6
- base_weight: bfloat16 [28672, 8192], P('fsdp'), may hold values from -0.0625 to 0.0625
- adapt_a: float32 [28672, 16], P('fsdp'), may hold values from -1.5 to 1.5
- adapt_b: float32 [16, 8192], P(None, 'fsdp'), may hold values from -0.0625 to 0.0625
- delta_vals: float32 [1024, 64, 64], P('fsdp'), may hold values from -0.75 to 0.75
- blk_row: int32 [1024], P('fsdp'), may hold values from 0 to 6, as said below
- blk_col: int32 [1024], P('fsdp'), may hold values from 0 to 127
- blk_count: int32 [64], P('fsdp'), may hold values from 1 to 16, as said below
Outputs:
- grad_hidden: bfloat16 [4096, 28672], P('dp', 'fsdp')
- grad_a: float32 [28672, 16], P('fsdp')
- grad_b: float32 [16, 8192], P(None, 'fsdp')
- grad_delta: float32 [1024, 64, 64], P('fsdp')
The draws below stay inside these ranges and needn't reach their ends.
Inputs may be any that keep to these rules, and one draw needn't show every extreme that they name: `blk_row`: each owner's slots name distinct blocks of its stripe. `blk_count`: some owner has all 16 slots live.
All inputs are finite; a program needn't handle non-finite values.
Results may differ from the reference program's by a relative error of at most 0.0013.
Values may be sent and summed in bfloat16 or wider, within the bound.
A program may use at most 32 MiB of HBM per device.

```python
import jax
import jax.numpy as jnp
from jax import lax

D = 8192
FFW = 28672
RANK = 16
BLK = 64
CAP = 16
TOKENS = 4096
NBLK = 1024
N_FSDP = 64


def block_layout(key):
    stripe = FFW // N_FSDP // BLK
    col_blocks = D // BLK
    owner_keys = jax.random.split(key, N_FSDP)

    def one_owner(owner_key):
        return jax.random.permutation(owner_key, stripe * col_blocks)[:CAP]
    return jax.vmap(one_owner)(owner_keys).reshape(-1).astype(jnp.int32)


def draw_blk_row(key, part):
    return block_layout(key) // (D // BLK)


def draw_blk_col(key, part):
    return block_layout(key) % (D // BLK)


def draw_blk_count(key, part):
    key = jax.random.fold_in(key, 7)
    first, second = jax.random.split(key)
    counts = jax.random.randint(first, (N_FSDP,), 1, CAP + 1).astype(jnp.int32)
    where_full = jax.random.randint(second, (), 0, N_FSDP)
    return counts.at[where_full].set(CAP)


def block_levels(own_key, dims, cuts, low, high):
    level = 1.0
    for dim, shards_of in cuts:
        heights = jax.random.uniform(jax.random.fold_in(jax.random.fold_in(own_key, 6), dim), (shards_of,), jnp.float32, low / len(cuts), high / len(cuts))
        level = level * jnp.repeat(jnp.exp(heights), dims[dim] // shards_of).reshape((-1,) + (1,) * (len(dims) - 1 - dim))
    return level


def centred(own_key, dims, scale, reach, pieces=(), kind=jnp.bfloat16):
    array = scale * jax.random.normal(own_key, dims, jnp.float32)
    if pieces:
        array = array * block_levels(own_key, dims, pieces, -0.22, 0.18)
    return jnp.clip(array, -reach, reach).astype(kind)


def setup_inputs(seed: int = 0) -> dict:
    key_list = jax.random.split(jax.random.key(seed), 10)
    grad_out = centred(key_list[0], (TOKENS, D), 1.0, 6.0, ((0, 16), (1, 64)))
    hidden = centred(key_list[1], (TOKENS, FFW), 1.0, 6.0, ((0, 16), (1, 64)))
    base_weight = centred(key_list[2], (FFW, D), D ** -0.5, 0.0625, ((0, 64),))
    adapt_a = centred(key_list[3], (FFW, RANK), 0.25, 1.5, ((0, 64),), jnp.float32)
    adapt_b = centred(key_list[4], (RANK, D), D ** -0.5, 0.0625, ((1, 64),), jnp.float32)
    delta_vals = centred(key_list[5], (NBLK, BLK, BLK), 0.125, 0.75, ((0, 64),), jnp.float32)
    blk_row = draw_blk_row(jax.random.fold_in(key_list[9], 71), 0)
    blk_col = draw_blk_col(jax.random.fold_in(key_list[9], 71), 0)
    blk_count = draw_blk_count(jax.random.fold_in(key_list[9], 71), 0)
    return dict(grad_out=grad_out, hidden=hidden, base_weight=base_weight, adapt_a=adapt_a, adapt_b=adapt_b, delta_vals=delta_vals, blk_row=blk_row, blk_col=blk_col, blk_count=blk_count)


def reference(grad_out, hidden, base_weight, adapt_a, adapt_b, delta_vals, blk_row, blk_col, blk_count):
    highest = lax.Precision.HIGHEST
    stripe = FFW // N_FSDP // BLK
    gy_wide = grad_out.astype(jnp.float32)
    h_wide = hidden.astype(jnp.float32)
    dense = jnp.dot(grad_out, base_weight.T, preferred_element_type=jnp.float32)
    gy_b = jnp.dot(gy_wide, adapt_b.T, precision=highest)
    h_a = jnp.dot(h_wide, adapt_a, precision=highest)
    slots = jnp.arange(N_FSDP * CAP, dtype=jnp.int32)
    owner = slots // CAP
    live = ((slots % CAP) < blk_count[owner]).astype(jnp.float32)
    glob_row = ((owner * stripe + blk_row) * BLK).astype(jnp.int32)
    glob_col = (blk_col * BLK).astype(jnp.int32)

    def step(sparse, item):
        row_start, col_start, values, flag = item
        cols = lax.dynamic_slice_in_dim(grad_out, col_start, BLK, 1)
        rows = lax.dynamic_slice_in_dim(hidden, row_start, BLK, 1)
        grad_blk = jnp.dot(rows.T, cols, preferred_element_type=jnp.float32) * flag
        contrib = jnp.dot(cols.astype(jnp.float32), values.T, precision=highest) * flag
        before = lax.dynamic_slice_in_dim(sparse, row_start, BLK, 1)
        sparse = lax.dynamic_update_slice_in_dim(sparse, before + contrib, row_start, 1)
        return sparse, grad_blk

    start = jnp.zeros((grad_out.shape[0], FFW), jnp.float32)
    sparse, grad_delta = lax.scan(step, start, (glob_row, glob_col, delta_vals, live))
    grad_hidden = (dense + jnp.dot(gy_b, adapt_a.T, precision=highest) + sparse).astype(jnp.bfloat16)
    grad_a = jnp.dot(h_wide.T, gy_b, precision=highest)
    grad_b = jnp.dot(h_a.T, gy_wide, precision=highest)
    return grad_hidden, grad_a, grad_b, grad_delta
```

```python
import jax
import jax.numpy as jnp
from jax import lax
from jax.experimental import pallas as pl
from jax.experimental.pallas import tpu as pltpu
from jax.sharding import PartitionSpec as P

MESH = pl.DeviceIdType.MESH
BF16, F32 = jnp.bfloat16, jnp.float32
HIGHEST = lax.Precision.HIGHEST
OFFSETS = (0, 1, -1, 2, -2, 3, -3, 4)
CHUNKS = ((0, 1, 0), (1, 2, 1), (3, 2, 2), (5, 2, 3), (7, 1, 4))
BOTH = tuple((half, way) for way in (0, 1) for half in (0, 1))
STEP = (1, -1)
HOP = {1: 1, 2: 2, 3: 1, 4: 2}


def ring_slot(step, distance):
    if distance in (0, 4):
        return 0 if distance == 0 else 7
    return 2 * distance - 1 if step == -1 else 2 * distance


def slot_of(offset):
    return jnp.where(offset == 0, 0, jnp.where(offset <= 4, 2 * offset - 1, 16 - 2 * offset))


def nt(a, b):
    return lax.dot_general(a, b, (((1,), (1,)), ((), ())), preferred_element_type=F32)


def nn(a, b):
    return lax.dot_general(a, b, (((1,), (0,)), ((), ())), preferred_element_type=F32)


def pieces(value):
    first = value.astype(BF16)
    rest = value - first.astype(F32)
    second = rest.astype(BF16)
    third = (rest - second.astype(F32)).astype(BF16)
    return first, second, third


def exact(product, value, other):
    return sum(product(piece, other) for piece in pieces(value)[::-1])


def kernel(
    gy_hbm, ht_hbm, w_hbm, at_hbm, b_hbm, vals_hbm, row_ref, col_ref, count_ref,
    gh_out, ga_out, gb_out, gd_out,
    buf, gy_v, ht_v, w_v, at_v, b_v, vals_v, load_sem,
    acc, spread, chosen,
    ring_send, ring_recv, bulk_send, bulk_recv,
    small, small_1, small_2, small_3, small_all, small_send, small_recv,
    sums, sums_core, sums_half, sums_y, sums_all, sums_send, sums_recv,
):
    f = lax.axis_index("fsdp")
    d = lax.axis_index("dp")
    x, z, y, core = f // 8, f % 8, d // 2, d % 2

    def along_x(k):
        return ((x + k + 8) % 8 * 8 + z, d)

    def along_z(k):
        return (x * 8 + (z + k + 8) % 8, d)

    def along_y(k):
        return (f, (y + k + 8) % 8 * 2 + core)

    other_core = (f, y * 2 + 1 - core)

    def first_axis(half, k):
        return along_z(k) if half else along_x(k)

    def second_axis(half, k):
        return along_x(k) if half else along_z(k)

    barrier = pltpu.get_barrier_semaphore()
    peers = [way(k) for way in (along_x, along_z, along_y) for k in range(1, 8)] + [other_core]
    for peer in peers:
        pl.semaphore_signal(barrier, inc=1, device_id=peer, device_id_type=MESH)

    loads = {
        "gy0": pltpu.make_async_copy(gy_hbm.at[pl.ds(0, 128)], buf.at[0, 0, 0], load_sem.at[0]),
        "gy1": pltpu.make_async_copy(gy_hbm.at[pl.ds(128, 128)], buf.at[1, 0, 0], load_sem.at[1]),
        "gy": pltpu.make_async_copy(gy_hbm, gy_v, load_sem.at[2]),
        "ht": pltpu.make_async_copy(ht_hbm, ht_v, load_sem.at[3]),
        "at": pltpu.make_async_copy(at_hbm, at_v, load_sem.at[4]),
        "b": pltpu.make_async_copy(b_hbm, b_v, load_sem.at[5]),
        "vals": pltpu.make_async_copy(vals_hbm, vals_v, load_sem.at[6]),
        "w": pltpu.make_async_copy(w_hbm, w_v, load_sem.at[7]),
    }
    for load in loads.values():
        load.start()
    loads["gy0"].wait()
    loads["gy1"].wait()
    pl.semaphore_wait(barrier, len(peers))

    sent = []

    def send(copy):
        copy.start()
        sent.append(copy)

    def ring(half, way, distance):
        step = STEP[way]
        source, target = ring_slot(step, distance - HOP[distance]), ring_slot(step, distance)
        rows = pl.ds(0, 128) if distance < 4 else pl.ds(way * 64, 64)
        return pltpu.make_async_remote_copy(
            buf.at[half, source, 0, rows], buf.at[half, target, 0, rows],
            ring_send.at[half, way, distance - 1], ring_recv.at[half, way, distance - 1],
            device_id=first_axis(half, step * HOP[distance]), device_id_type=MESH,
        )

    def bulk(half, way, hop, chunk):
        step = STEP[way]
        source, target = ring_slot(step, hop), ring_slot(step, hop + 1)
        rows = pl.ds(0, 128) if hop < 3 else pl.ds(way * 64, 64)
        slots = pl.ds(CHUNKS[chunk][0], CHUNKS[chunk][1])
        return pltpu.make_async_remote_copy(
            buf.at[half, slots, source, rows], buf.at[half, slots, target, rows],
            bulk_send.at[half, way, hop, chunk], bulk_recv.at[half, way, hop, chunk],
            device_id=second_axis(half, step), device_id_type=MESH,
        )

    def ring_arrive(distance):
        for half, way in BOTH:
            ring(half, way, distance).wait_recv()
            for later in (3, 4):
                if later - HOP[later] == distance:
                    send(ring(half, way, later))
        for chunk, entry in enumerate(CHUNKS):
            if entry[2] == distance:
                for half, way in BOTH:
                    send(bulk(half, way, 0, chunk))

    def bulk_arrive(hop, chunk):
        for half, way in BOTH:
            bulk(half, way, hop, chunk).wait_recv()
            if hop < 3:
                send(bulk(half, way, hop + 1, chunk))

    def dense(half, slot):
        across = OFFSETS[slot]
        weight, blocks = [], []
        for other in range(8):
            along = OFFSETS[other]
            if half == 0:
                owner = (x + along + 8) % 8 * 8 + (z + across + 8) % 8
            else:
                owner = (x + across + 8) % 8 * 8 + (z + along + 8) % 8
            weight.append(w_v[:, pl.ds(pl.multiple_of(owner * 128, 128), 128)])
            blocks.append(buf[half, other, slot])
        part = nt(jnp.concatenate(weight, axis=1), jnp.concatenate(blocks, axis=1))
        place = pl.ds(half * 128, 128)
        acc[:, place] = part if slot == 0 else acc[:, place] + part

    def small_copy(stage, k):
        source, target, peer = (
            (small.at[(x + k) % 8], small_1.at[k], along_x(k)),
            (small_2.at[0], small_2.at[k], along_z(k)),
            (small_3.at[0], small_3.at[k], along_x(k)),
        )[stage]
        return pltpu.make_async_remote_copy(
            source, target, small_send.at[stage, k], small_recv.at[stage, k],
            device_id=peer, device_id_type=MESH,
        )

    def small_start():
        for name in ("gy", "ht", "at", "b"):
            loads[name].wait()
        part_gb = exact(nt, b_v[...], gy_v[...])
        part_ha = exact(nn, at_v[...], ht_v[...].reshape(448, 256))
        for piece in range(8):
            group, side = piece // 2, piece % 2
            source = part_gb if group < 2 else part_ha
            small[piece] = source[group % 2 * 8 : group % 2 * 8 + 8, side * 128 : side * 128 + 128]
        for k in range(1, 8):
            send(small_copy(0, k))

    def small_second():
        for k in range(1, 8):
            small_copy(0, k).wait_recv()
        total = small[x]
        for k in range(1, 8):
            total = total + small_1[k]
        small_2[0] = total
        for k in range(1, 8):
            send(small_copy(1, k))

    def small_third():
        for k in range(1, 8):
            small_copy(1, k).wait_recv()
        total = small_2[0]
        for k in range(1, 8):
            total = total + small_2[k]
        small_3[0] = total
        for k in range(1, 8):
            send(small_copy(2, k))

    def small_end():
        small_all[x] = small_3[0]
        for k in range(1, 8):
            small_copy(2, k).wait_recv()
            small_all[(x + 8 - k) % 8] = small_3[k]
        rows = [
            jnp.concatenate([small_all[2 * group], small_all[2 * group + 1]], axis=1)
            for group in range(4)
        ]
        gy_b = jnp.concatenate(rows[:2], axis=0)
        h_a = jnp.concatenate(rows[2:], axis=0)
        grad_a = exact(nt, gy_b, ht_v[...].reshape(448, 256))
        grad_b = exact(nn, h_a, gy_v[...])
        wide = jnp.concatenate([grad_a, jnp.zeros((16, 64), F32), grad_b], axis=1)
        for tile in range(16):
            if tile < 10:
                group, lane = tile // 5, tile % 5 * 128
                value = wide[group * 8 : group * 8 + 8, lane : lane + 128]
            else:
                value = jnp.zeros((8, 128), F32)
            sums[tile // 2, tile % 2, 32:40] = value
        adapter = lax.dot_general(
            at_v[...], gy_b, (((0,), (0,)), ((), ())), precision=HIGHEST,
            preferred_element_type=F32,
        )
        acc[...] += adapter

    def spread_deltas():
        loads["vals"].wait()
        live_slots = count_ref[0]
        side = lax.broadcasted_iota(jnp.int32, (64, 128), 1) // 64
        for k in range(16):
            value = vals_v[k]
            keep = (side == col_ref[k] % 2) & (live_slots > k)
            value = jnp.where(keep, jnp.concatenate([value, value], axis=1), 0.0)
            first, second, _ = pieces(value)
            place = pl.ds(k * 128, 128)
            for block in range(7):
                here = row_ref[k] == block
                rows = pl.ds(block * 64, 64)
                spread[0, rows, place] = jnp.where(here, first, jnp.zeros_like(first))
                spread[1, rows, place] = jnp.where(here, second, jnp.zeros_like(second))

    def choose():
        for k in range(16):
            owner = col_ref[k] // 2
            slot_x = slot_of((owner // 8 - x + 8) % 8)
            slot_z = slot_of((owner % 8 - z + 8) % 8)
            place = pl.ds(k * 128, 128)
            chosen[0:128, place] = buf[0, slot_x, slot_z]
            chosen[128:256, place] = buf[1, slot_z, slot_x]

    def grad_deltas():
        live_slots = count_ref[0]
        lane = lax.broadcasted_iota(jnp.int32, (64, 128), 1)
        for pair in range(8):
            sides = []
            for k in (pair, pair + 8):
                block = nn(ht_v[row_ref[k]], chosen[:, k * 128 : k * 128 + 128])
                block = jnp.where(live_slots > k, block, 0.0)
                swap = (col_ref[k] % 2) != (k // 8)
                sides.append(jnp.where(swap, pltpu.roll(block, 64, 1), block))
            both = jnp.where(lane < 64, sides[0], sides[1])
            sums[pair, 0, 0:32] = both[0:32]
            sums[pair, 1, 0:32] = both[32:64]

    def sums_copy(stage, k):
        source, target, peer = (
            lambda: (sums.at[:, 1 - core], sums_core, other_core),
            lambda: (sums_half.at[(y + k) % 8], sums_y.at[k], along_y(k)),
            lambda: (sums_all.at[y, core], sums_all.at[y, core], along_y(k)),
            lambda: (sums_all.at[(y + 8 - k) % 8, core], sums_all.at[(y + 8 - k) % 8, core], other_core),
        )[stage]()
        return pltpu.make_async_remote_copy(
            source, target, sums_send.at[stage, k], sums_recv.at[stage, k],
            device_id=peer, device_id_type=MESH,
        )

    for half, way in BOTH:
        send(ring(half, way, 1))
    for half, way in BOTH:
        send(bulk(half, way, 0, 0))
    for half, way in BOTH:
        send(ring(half, way, 2))
    small_start()

    ring_arrive(1)
    ring_arrive(2)
    bulk_arrive(0, 0)
    small_second()

    ring_arrive(3)
    ring_arrive(4)
    bulk_arrive(1, 0)
    bulk_arrive(0, 1)
    bulk_arrive(0, 2)
    small_third()
    loads["w"].wait()
    dense(0, 0)
    dense(1, 0)

    for wave in range(2, 6):
        for chunk in range(5):
            hop = wave - (0, 1, 1, 2, 2)[chunk]
            if hop < 4:
                bulk_arrive(hop, chunk)
        if wave == 2:
            small_end()
            spread_deltas()
        hop = wave - 2
        if hop < 3:
            for half, way in BOTH:
                dense(half, ring_slot(STEP[way], hop + 1))

    choose()
    grad_deltas()
    send(sums_copy(0, 0))
    dense(0, 7)
    dense(1, 7)
    sums_copy(0, 0).wait_recv()
    sums_half[...] = sums[:, core] + sums_core[...]
    for k in range(1, 8):
        send(sums_copy(1, k))
    total = acc[...]
    for part in (1, 0):
        total = total + nt(spread[part], chosen[...])
    gh_out[...] = total.astype(BF16)
    total = sums_half[y]
    for k in range(1, 8):
        sums_copy(1, k).wait_recv()
        total = total + sums_y[k]
    sums_all[y, core] = total
    for k in range(1, 8):
        send(sums_copy(2, k))
    send(sums_copy(3, 0))
    for k in range(1, 8):
        sums_copy(2, k).wait_recv()
        send(sums_copy(3, k))
    for k in range(8):
        sums_copy(3, k).wait_recv()
    for pair in range(8):
        for side in (0, 1):
            value = sums_all[pair, side]
            rows = pl.ds(side * 32, 32)
            gd_out[pair, rows] = value[0:32, 0:64]
            gd_out[pair + 8, rows] = value[0:32, 64:128]
            tile = 2 * pair + side
            if tile < 10:
                group, lane = pl.ds(tile // 5 * 8, 8), tile % 5
                if lane < 3:
                    ga_out[group, lane * 128 : lane * 128 + 128] = value[32:40]
                elif lane == 3:
                    ga_out[group, 384:448] = value[32:40, 0:64]
                else:
                    gb_out[group, :] = value[32:40]
    for copy in sent:
        copy.wait_send()


def on_device(
    grad_out, hidden, base_weight, adapt_a, adapt_b, delta_vals, blk_row, blk_col, blk_count
):
    hbm = pl.BlockSpec(memory_space=pltpu.HBM)
    scalar = pl.BlockSpec(memory_space=pltpu.SMEM)
    vmem = pl.BlockSpec(memory_space=pltpu.VMEM)
    dma = pltpu.SemaphoreType.DMA
    gh, ga, gb, gd = pl.pallas_call(
        kernel,
        out_shape=(
            jax.ShapeDtypeStruct((448, 256), BF16),
            jax.ShapeDtypeStruct((16, 448), F32),
            jax.ShapeDtypeStruct((16, 128), F32),
            jax.ShapeDtypeStruct((16, 64, 64), F32),
        ),
        in_specs=[hbm] * 6 + [scalar] * 3,
        out_specs=(vmem,) * 4,
        scratch_shapes=[
            pltpu.VMEM((2, 8, 8, 128, 128), BF16),
            pltpu.VMEM((256, 128), BF16),
            pltpu.VMEM((7, 64, 256), BF16),
            pltpu.VMEM((448, 8192), BF16),
            pltpu.VMEM((16, 448), F32),
            pltpu.VMEM((16, 128), F32),
            pltpu.VMEM((16, 64, 64), F32),
            dma((8,)),
            pltpu.VMEM((448, 256), F32),
            pltpu.VMEM((2, 448, 2048), BF16),
            pltpu.VMEM((256, 2048), BF16),
            dma((2, 2, 4)),
            dma((2, 2, 4)),
            dma((2, 2, 4, 5)),
            dma((2, 2, 4, 5)),
            pltpu.VMEM((8, 8, 128), F32),
            pltpu.VMEM((8, 8, 128), F32),
            pltpu.VMEM((8, 8, 128), F32),
            pltpu.VMEM((8, 8, 128), F32),
            pltpu.VMEM((8, 8, 128), F32),
            dma((3, 8)),
            dma((3, 8)),
            pltpu.VMEM((8, 2, 40, 128), F32),
            pltpu.VMEM((8, 40, 128), F32),
            pltpu.VMEM((8, 40, 128), F32),
            pltpu.VMEM((8, 40, 128), F32),
            pltpu.VMEM((8, 2, 40, 128), F32),
            dma((4, 8)),
            dma((4, 8)),
        ],
        compiler_params=pltpu.CompilerParams(
            collective_id=0, has_side_effects=True, vmem_limit_bytes=60 << 20
        ),
        cost_estimate=pl.CostEstimate(
            flops=3_000_000_000, bytes_accessed=12_000_000, transcendentals=0
        ),
    )(
        grad_out, hidden.T.reshape(7, 64, 256), base_weight, adapt_a.T, adapt_b, delta_vals,
        blk_row, blk_col, blk_count,
    )
    return gh.T, ga.T, gb, gd


def solution(mesh):
    placed = (
        P("dp", "fsdp"),
        P("dp", "fsdp"),
        P("fsdp", None),
        P("fsdp", None),
        P(None, "fsdp"),
        P("fsdp", None, None),
        P("fsdp"),
        P("fsdp"),
        P("fsdp"),
    )
    return jax.shard_map(
        on_device,
        mesh=mesh,
        in_specs=placed,
        out_specs=(P("dp", "fsdp"), P("fsdp", None), P(None, "fsdp"), P("fsdp", None, None)),
        check_vma=False,
    )
```

```python
import jax
import jax.numpy as jnp
from jax import lax
from jax.experimental import pallas as pl
from jax.experimental.pallas import tpu as pltpu
from jax.sharding import PartitionSpec as P

MESH = pl.DeviceIdType.MESH
BF16, F32 = jnp.bfloat16, jnp.float32
HIGHEST = lax.Precision.HIGHEST
OFFSETS = (0, 1, -1, 2, -2, 3, -3, 4)
CHUNKS = ((0, 1, 0), (1, 2, 1), (3, 2, 2), (5, 2, 3), (7, 1, 4))
BOTH = tuple((half, way) for way in (0, 1) for half in (0, 1))
STEP = (1, -1)
HOP = {1: 1, 2: 2, 3: 1, 4: 2}


def ring_slot(step, distance):
    if distance in (0, 4):
        return 0 if distance == 0 else 7
    return 2 * distance - 1 if step == -1 else 2 * distance


def slot_of(offset):
    return jnp.where(offset == 0, 0, jnp.where(offset <= 4, 2 * offset - 1, 16 - 2 * offset))


def nt(a, b):
    return lax.dot_general(a, b, (((1,), (1,)), ((), ())), preferred_element_type=F32)


def nn(a, b):
    return lax.dot_general(a, b, (((1,), (0,)), ((), ())), preferred_element_type=F32)


def pieces(value):
    first = value.astype(BF16)
    rest = value - first.astype(F32)
    second = rest.astype(BF16)
    third = (rest - second.astype(F32)).astype(BF16)
    return first, second, third


def exact(product, value, other):
    return sum(product(piece, other) for piece in pieces(value)[::-1])


def kernel(
    gy_hbm, ht_hbm, w_hbm, at_hbm, b_hbm, vals_hbm, row_ref, col_ref, count_ref,
    gh_out, sums_out,
    buf, gy_v, ht_v, w_v, at_v, b_v, vals_v, load_sem,
    acc, spread, chosen, gh_v,
    ring_send, ring_recv, bulk_send, bulk_recv,
    small, small_1, small_2, small_3, small_all, small_send, small_recv,
    sums, sums_core, sums_half, sums_y, sums_all, sums_send, sums_recv,
):
    f = lax.axis_index("fsdp")
    d = lax.axis_index("dp")
    x, z, y, core = f // 8, f % 8, d // 2, d % 2

    def along_x(k):
        return ((x + k + 8) % 8 * 8 + z, d)

    def along_z(k):
        return (x * 8 + (z + k + 8) % 8, d)

    def along_y(k):
        return (f, (y + k + 8) % 8 * 2 + core)

    other_core = (f, y * 2 + 1 - core)

    def first_axis(half, k):
        return along_z(k) if half else along_x(k)

    def second_axis(half, k):
        return along_x(k) if half else along_z(k)

    barrier = pltpu.get_barrier_semaphore()
    peers = [way(k) for way in (along_x, along_z, along_y) for k in range(1, 8)] + [other_core]
    for peer in peers:
        pl.semaphore_signal(barrier, inc=1, device_id=peer, device_id_type=MESH)

    loads = {
        "gy0": pltpu.make_async_copy(gy_hbm.at[pl.ds(0, 128)], buf.at[0, 0, 0], load_sem.at[0]),
        "gy1": pltpu.make_async_copy(gy_hbm.at[pl.ds(128, 128)], buf.at[1, 0, 0], load_sem.at[1]),
        "gy": pltpu.make_async_copy(gy_hbm, gy_v, load_sem.at[2]),
        "ht": pltpu.make_async_copy(ht_hbm, ht_v, load_sem.at[3]),
        "at": pltpu.make_async_copy(at_hbm, at_v, load_sem.at[4]),
        "b": pltpu.make_async_copy(b_hbm, b_v, load_sem.at[5]),
        "vals": pltpu.make_async_copy(vals_hbm, vals_v, load_sem.at[6]),
        "w": pltpu.make_async_copy(w_hbm, w_v, load_sem.at[7]),
    }
    for load in loads.values():
        load.start()
    loads["gy0"].wait()
    loads["gy1"].wait()
    pl.semaphore_wait(barrier, len(peers))

    sent = []

    def send(copy):
        copy.start()
        sent.append(copy)

    def ring(half, way, distance):
        step = STEP[way]
        source, target = ring_slot(step, distance - HOP[distance]), ring_slot(step, distance)
        rows = pl.ds(0, 128) if distance < 4 else pl.ds(way * 64, 64)
        return pltpu.make_async_remote_copy(
            buf.at[half, source, 0, rows], buf.at[half, target, 0, rows],
            ring_send.at[half, way, distance - 1], ring_recv.at[half, way, distance - 1],
            device_id=first_axis(half, step * HOP[distance]), device_id_type=MESH,
        )

    def bulk(half, way, hop, chunk):
        step = STEP[way]
        source, target = ring_slot(step, hop), ring_slot(step, hop + 1)
        rows = pl.ds(0, 128) if hop < 3 else pl.ds(way * 64, 64)
        slots = pl.ds(CHUNKS[chunk][0], CHUNKS[chunk][1])
        return pltpu.make_async_remote_copy(
            buf.at[half, slots, source, rows], buf.at[half, slots, target, rows],
            bulk_send.at[half, way, hop, chunk], bulk_recv.at[half, way, hop, chunk],
            device_id=second_axis(half, step), device_id_type=MESH,
        )

    def ring_arrive(distance):
        for half, way in BOTH:
            ring(half, way, distance).wait_recv()
            for later in (3, 4):
                if later - HOP[later] == distance:
                    send(ring(half, way, later))
        for chunk, entry in enumerate(CHUNKS):
            if entry[2] == distance:
                for half, way in BOTH:
                    send(bulk(half, way, 0, chunk))

    def bulk_arrive(hop, chunk):
        for half, way in BOTH:
            bulk(half, way, hop, chunk).wait_recv()
            if hop < 3:
                send(bulk(half, way, hop + 1, chunk))

    def dense(half, slot):
        across = OFFSETS[slot]
        weight, blocks = [], []
        for other in range(8):
            along = OFFSETS[other]
            if half == 0:
                owner = (x + along + 8) % 8 * 8 + (z + across + 8) % 8
            else:
                owner = (x + across + 8) % 8 * 8 + (z + along + 8) % 8
            weight.append(w_v[:, pl.ds(pl.multiple_of(owner * 128, 128), 128)])
            blocks.append(buf[half, other, slot])
        part = nt(jnp.concatenate(weight, axis=1), jnp.concatenate(blocks, axis=1))
        place = pl.ds(half * 128, 128)
        acc[:, place] = part if slot == 0 else acc[:, place] + part

    def small_copy(stage, k):
        source, target, peer = (
            (small.at[(x + k) % 8], small_1.at[k], along_x(k)),
            (small_2.at[0], small_2.at[k], along_z(k)),
            (small_3.at[0], small_3.at[k], along_x(k)),
        )[stage]
        return pltpu.make_async_remote_copy(
            source, target, small_send.at[stage, k], small_recv.at[stage, k],
            device_id=peer, device_id_type=MESH,
        )

    def small_start():
        for name in ("gy", "ht", "at", "b"):
            loads[name].wait()
        part_gb = exact(nt, b_v[...], gy_v[...])
        part_ha = exact(nn, at_v[...], ht_v[...].reshape(448, 256))
        for piece in range(8):
            group, side = piece // 2, piece % 2
            source = part_gb if group < 2 else part_ha
            small[piece] = source[group % 2 * 8 : group % 2 * 8 + 8, side * 128 : side * 128 + 128]
        for k in range(1, 8):
            send(small_copy(0, k))

    def small_second():
        for k in range(1, 8):
            small_copy(0, k).wait_recv()
        total = small[x]
        for k in range(1, 8):
            total = total + small_1[k]
        small_2[0] = total
        for k in range(1, 8):
            send(small_copy(1, k))

    def small_third():
        for k in range(1, 8):
            small_copy(1, k).wait_recv()
        total = small_2[0]
        for k in range(1, 8):
            total = total + small_2[k]
        small_3[0] = total
        for k in range(1, 8):
            send(small_copy(2, k))

    def small_end():
        small_all[x] = small_3[0]
        for k in range(1, 8):
            small_copy(2, k).wait_recv()
            small_all[(x + 8 - k) % 8] = small_3[k]
        rows = [
            jnp.concatenate([small_all[2 * group], small_all[2 * group + 1]], axis=1)
            for group in range(4)
        ]
        gy_b = jnp.concatenate(rows[:2], axis=0)
        h_a = jnp.concatenate(rows[2:], axis=0)
        grad_a = exact(nt, gy_b, ht_v[...].reshape(448, 256))
        grad_b = exact(nn, h_a, gy_v[...])
        wide = jnp.concatenate([grad_a, jnp.zeros((16, 64), F32), grad_b], axis=1)
        for tile in range(16):
            if tile < 10:
                group, lane = tile // 5, tile % 5 * 128
                value = wide[group * 8 : group * 8 + 8, lane : lane + 128]
            else:
                value = jnp.zeros((8, 128), F32)
            sums[tile // 2, tile % 2, 32:40] = value
        adapter = lax.dot_general(
            at_v[...], gy_b, (((0,), (0,)), ((), ())), precision=HIGHEST,
            preferred_element_type=F32,
        )
        acc[...] += adapter

    def spread_deltas():
        loads["vals"].wait()
        live_slots = count_ref[0]
        side = lax.broadcasted_iota(jnp.int32, (64, 128), 1) // 64
        for k in range(16):
            value = vals_v[k]
            keep = (side == col_ref[k] % 2) & (live_slots > k)
            value = jnp.where(keep, jnp.concatenate([value, value], axis=1), 0.0)
            first, second, _ = pieces(value)
            place = pl.ds(k * 128, 128)
            for block in range(7):
                here = row_ref[k] == block
                rows = pl.ds(block * 64, 64)
                spread[0, rows, place] = jnp.where(here, first, jnp.zeros_like(first))
                spread[1, rows, place] = jnp.where(here, second, jnp.zeros_like(second))

    def choose():
        for k in range(16):
            owner = col_ref[k] // 2
            slot_x = slot_of((owner // 8 - x + 8) % 8)
            slot_z = slot_of((owner % 8 - z + 8) % 8)
            place = pl.ds(k * 128, 128)
            chosen[0:128, place] = buf[0, slot_x, slot_z]
            chosen[128:256, place] = buf[1, slot_z, slot_x]

    def grad_deltas():
        live_slots = count_ref[0]
        lane = lax.broadcasted_iota(jnp.int32, (64, 128), 1)
        for pair in range(8):
            sides = []
            for k in (pair, pair + 8):
                block = nn(ht_v[row_ref[k]], chosen[:, k * 128 : k * 128 + 128])
                block = jnp.where(live_slots > k, block, 0.0)
                swap = (col_ref[k] % 2) != (k // 8)
                sides.append(jnp.where(swap, pltpu.roll(block, 64, 1), block))
            both = jnp.where(lane < 64, sides[0], sides[1])
            sums[pair, 0, 0:32] = both[0:32]
            sums[pair, 1, 0:32] = both[32:64]

    def sums_copy(stage, k):
        source, target, peer = (
            lambda: (sums.at[:, 1 - core], sums_core, other_core),
            lambda: (sums_half.at[(y + k) % 8], sums_y.at[k], along_y(k)),
            lambda: (sums_all.at[y, core], sums_all.at[y, core], along_y(k)),
            lambda: (sums_all.at[(y + 8 - k) % 8, core], sums_all.at[(y + 8 - k) % 8, core], other_core),
        )[stage]()
        return pltpu.make_async_remote_copy(
            source, target, sums_send.at[stage, k], sums_recv.at[stage, k],
            device_id=peer, device_id_type=MESH,
        )

    for half, way in BOTH:
        send(ring(half, way, 1))
    for half, way in BOTH:
        send(bulk(half, way, 0, 0))
    for half, way in BOTH:
        send(ring(half, way, 2))
    small_start()

    ring_arrive(1)
    ring_arrive(2)
    bulk_arrive(0, 0)

    ring_arrive(3)
    ring_arrive(4)
    bulk_arrive(1, 0)
    bulk_arrive(0, 1)
    bulk_arrive(0, 2)
    small_second()
    loads["w"].wait()
    dense(0, 0)
    dense(1, 0)

    for wave in range(2, 6):
        for chunk in range(5):
            hop = wave - (0, 1, 1, 2, 2)[chunk]
            if hop < 4:
                bulk_arrive(hop, chunk)
        if wave == 2:
            spread_deltas()
        if wave == 3:
            small_third()
        hop = wave - 2
        if hop < 3:
            for half, way in BOTH:
                dense(half, ring_slot(STEP[way], hop + 1))
        if wave == 4:
            small_end()

    choose()
    grad_deltas()
    send(sums_copy(0, 0))
    sums_copy(0, 0).wait_recv()
    sums_half[...] = sums[:, core] + sums_core[...]
    for k in range(1, 8):
        send(sums_copy(1, k))
    dense(0, 7)
    dense(1, 7)
    total = acc[...]
    for part in (1, 0):
        total = total + nt(spread[part], chosen[...])
    gh_v[...] = total.astype(BF16)
    gh_copy = pltpu.make_async_copy(gh_v, gh_out, load_sem.at[0])
    gh_copy.start()
    total = sums_half[y]
    for k in range(1, 8):
        sums_copy(1, k).wait_recv()
        total = total + sums_y[k]
    sums_all[y, core] = total
    for k in range(1, 8):
        send(sums_copy(2, k))
    send(sums_copy(3, 0))
    for k in range(1, 8):
        sums_copy(2, k).wait_recv()
        send(sums_copy(3, k))
    for k in range(8):
        sums_copy(3, k).wait_recv()
    sums_write = pltpu.make_async_copy(sums_all, sums_out, load_sem.at[1])
    sums_write.start()
    for copy in sent:
        copy.wait_send()
    gh_copy.wait()
    sums_write.wait()


def finish(gh_in, sums_in, gh_out, ga_out, gb_out, gd_out):
    gh_out[...] = gh_in[...]
    for pair in range(8):
        for side in (0, 1):
            value = sums_in[pair, side]
            rows = pl.ds(side * 32, 32)
            gd_out[pair, rows] = value[0:32, 0:64]
            gd_out[pair + 8, rows] = value[0:32, 64:128]
            tile = 2 * pair + side
            if tile < 10:
                group, lane = pl.ds(tile // 5 * 8, 8), tile % 5
                if lane < 3:
                    ga_out[group, lane * 128 : lane * 128 + 128] = value[32:40]
                elif lane == 3:
                    ga_out[group, 384:448] = value[32:40, 0:64]
                else:
                    gb_out[group, :] = value[32:40]


def on_device(
    grad_out, hidden, base_weight, adapt_a, adapt_b, delta_vals, blk_row, blk_col, blk_count
):
    hbm = pl.BlockSpec(memory_space=pltpu.HBM)
    scalar = pl.BlockSpec(memory_space=pltpu.SMEM)
    vmem = pl.BlockSpec(memory_space=pltpu.VMEM)
    dma = pltpu.SemaphoreType.DMA
    small_tiles = pltpu.VMEM((8, 8, 128), F32)
    gathered, summed = pl.pallas_call(
        kernel,
        out_shape=(
            jax.ShapeDtypeStruct((448, 256), BF16),
            jax.ShapeDtypeStruct((8, 2, 40, 128), F32),
        ),
        in_specs=[hbm] * 6 + [scalar] * 3,
        out_specs=(hbm, hbm),
        scratch_shapes=[
            pltpu.VMEM((2, 8, 8, 128, 128), BF16),
            pltpu.VMEM((256, 128), BF16),
            pltpu.VMEM((7, 64, 256), BF16),
            pltpu.VMEM((448, 8192), BF16),
            pltpu.VMEM((16, 448), F32),
            pltpu.VMEM((16, 128), F32),
            pltpu.VMEM((16, 64, 64), F32),
            dma((8,)),
            pltpu.VMEM((448, 256), F32),
            pltpu.VMEM((2, 448, 2048), BF16),
            pltpu.VMEM((256, 2048), BF16),
            pltpu.VMEM((448, 256), BF16),
            dma((2, 2, 4)),
            dma((2, 2, 4)),
            dma((2, 2, 4, 5)),
            dma((2, 2, 4, 5)),
            small_tiles,
            small_tiles,
            small_tiles,
            small_tiles,
            small_tiles,
            dma((3, 8)),
            dma((3, 8)),
            pltpu.VMEM((8, 2, 40, 128), F32),
            pltpu.VMEM((8, 40, 128), F32),
            pltpu.VMEM((8, 40, 128), F32),
            pltpu.VMEM((8, 40, 128), F32),
            pltpu.VMEM((8, 2, 40, 128), F32),
            dma((4, 8)),
            dma((4, 8)),
        ],
        compiler_params=pltpu.CompilerParams(
            collective_id=0, has_side_effects=True, vmem_limit_bytes=60 << 20
        ),
        cost_estimate=pl.CostEstimate(
            flops=3_000_000_000, bytes_accessed=12_000_000, transcendentals=0
        ),
    )(
        grad_out, hidden.T.reshape(7, 64, 256), base_weight, adapt_a.T, adapt_b, delta_vals,
        blk_row, blk_col, blk_count,
    )
    gh, ga, gb, gd = pl.pallas_call(
        finish,
        out_shape=(
            jax.ShapeDtypeStruct((448, 256), BF16),
            jax.ShapeDtypeStruct((16, 448), F32),
            jax.ShapeDtypeStruct((16, 128), F32),
            jax.ShapeDtypeStruct((16, 64, 64), F32),
        ),
        in_specs=[vmem] * 2,
        out_specs=(vmem,) * 4,
        compiler_params=pltpu.CompilerParams(vmem_limit_bytes=60 << 20),
    )(gathered, summed)
    return gh.T, ga.T, gb, gd


def solution(mesh):
    placed = (
        P("dp", "fsdp"),
        P("dp", "fsdp"),
        P("fsdp", None),
        P("fsdp", None),
        P(None, "fsdp"),
        P("fsdp", None, None),
        P("fsdp"),
        P("fsdp"),
        P("fsdp"),
    )
    return jax.shard_map(
        on_device,
        mesh=mesh,
        in_specs=placed,
        out_specs=(P("dp", "fsdp"), P("fsdp", None), P(None, "fsdp"), P("fsdp", None, None)),
        check_vma=False,
    )
```

```python
import jax
import jax.numpy as jnp
from jax import lax
from jax.experimental import pallas as pl
from jax.experimental.pallas import tpu as pltpu
from jax.sharding import PartitionSpec as P

MESH = pl.DeviceIdType.MESH
BF16, F32 = jnp.bfloat16, jnp.float32
HIGHEST = lax.Precision.HIGHEST
OFFSETS = (0, 1, -1, 2, -2, 3, -3, 4)
CHUNKS = ((0, 1, 0), (1, 2, 1), (3, 2, 2), (5, 2, 3), (7, 1, 4))
BOTH = tuple((half, way) for way in (0, 1) for half in (0, 1))
STEP = (1, -1)
FAR_FIRST = (4, 3, 5, 2, 6, 1, 7)
HOP = {1: 1, 2: 2, 3: 1, 4: 2}


def ring_slot(step, distance):
    if distance in (0, 4):
        return 0 if distance == 0 else 7
    return 2 * distance - 1 if step == -1 else 2 * distance


def slot_of(offset):
    return jnp.where(offset == 0, 0, jnp.where(offset <= 4, 2 * offset - 1, 16 - 2 * offset))


def nt(a, b):
    return lax.dot_general(a, b, (((1,), (1,)), ((), ())), preferred_element_type=F32)


def nn(a, b):
    return lax.dot_general(a, b, (((1,), (0,)), ((), ())), preferred_element_type=F32)


def pieces(value):
    first = value.astype(BF16)
    rest = value - first.astype(F32)
    second = rest.astype(BF16)
    third = (rest - second.astype(F32)).astype(BF16)
    return first, second, third


def exact(product, value, other):
    return sum(product(piece, other) for piece in pieces(value)[::-1])


def kernel(
    gy_hbm, ht_hbm, w_hbm, at_hbm, b_hbm, vals_hbm, row_ref, col_ref, count_ref,
    gh_out, sums_out,
    buf, gy_v, ht_v, w_v, at_v, b_v, vals_v, load_sem,
    acc, spread, chosen, gh_v,
    ring_send, ring_recv, bulk_send, bulk_recv, ready, ready_core,
    small, small_1, small_2, small_3, small_all, small_send, small_recv,
    sums, sums_core, sums_half, sums_y, sums_all, sums_send, sums_recv,
):
    f = lax.axis_index("fsdp")
    d = lax.axis_index("dp")
    x, z, y, core = f // 8, f % 8, d // 2, d % 2

    def along_x(k):
        return ((x + k + 8) % 8 * 8 + z, d)

    def along_z(k):
        return (x * 8 + (z + k + 8) % 8, d)

    def along_y(k):
        return (f, (y + k + 8) % 8 * 2 + core)

    other_core = (f, y * 2 + 1 - core)

    def first_axis(half, k):
        return along_z(k) if half else along_x(k)

    def second_axis(half, k):
        return along_x(k) if half else along_z(k)

    def at_z(other):
        return (x * 8 + other, d)

    def signal(semaphore, peer):
        pl.semaphore_signal(semaphore, inc=1, device_id=peer, device_id_type=MESH)

    barrier = pltpu.get_barrier_semaphore()
    for k in range(1, 8):
        signal(barrier, along_x(k))
        pl.when(z < k)(lambda k=k: signal(barrier, at_z(k)))
    for k in range(1, 8):
        signal(barrier, along_y(k))
    pl.when(core == 0)(lambda: signal(barrier, other_core))

    loads = {
        "gy0": pltpu.make_async_copy(gy_hbm.at[pl.ds(0, 128)], buf.at[0, 0, 0], load_sem.at[0]),
        "gy1": pltpu.make_async_copy(gy_hbm.at[pl.ds(128, 128)], buf.at[1, 0, 0], load_sem.at[1]),
        "gy": pltpu.make_async_copy(gy_hbm, gy_v, load_sem.at[2]),
        "ht": pltpu.make_async_copy(ht_hbm, ht_v, load_sem.at[3]),
        "at": pltpu.make_async_copy(at_hbm, at_v, load_sem.at[4]),
        "b": pltpu.make_async_copy(b_hbm, b_v, load_sem.at[5]),
        "vals": pltpu.make_async_copy(vals_hbm, vals_v, load_sem.at[6]),
        "w": pltpu.make_async_copy(w_hbm, w_v, load_sem.at[7]),
    }
    for load in loads.values():
        load.start()
    loads["gy0"].wait()
    loads["gy1"].wait()
    pl.semaphore_wait(barrier, 14 + z + core)
    for k in range(7):
        pl.when(z > k)(lambda k=k: signal(ready.at[z], at_z(k)))
    pl.when(core == 1)(lambda: signal(ready_core, other_core))

    sent = []

    def send(copy):
        copy.start()
        sent.append(copy)

    def ring(half, way, distance):
        step = STEP[way]
        source, target = ring_slot(step, distance - HOP[distance]), ring_slot(step, distance)
        rows = pl.ds(0, 128) if distance < 4 else pl.ds(way * 64, 64)
        return pltpu.make_async_remote_copy(
            buf.at[half, source, 0, rows], buf.at[half, target, 0, rows],
            ring_send.at[half, way, distance - 1], ring_recv.at[half, way, distance - 1],
            device_id=first_axis(half, step * HOP[distance]), device_id_type=MESH,
        )

    def bulk(half, way, hop, chunk):
        step = STEP[way]
        source, target = ring_slot(step, hop), ring_slot(step, hop + 1)
        rows = pl.ds(0, 128) if hop < 3 else pl.ds(way * 64, 64)
        slots = pl.ds(CHUNKS[chunk][0], CHUNKS[chunk][1])
        return pltpu.make_async_remote_copy(
            buf.at[half, slots, source, rows], buf.at[half, slots, target, rows],
            bulk_send.at[half, way, hop, chunk], bulk_recv.at[half, way, hop, chunk],
            device_id=second_axis(half, step), device_id_type=MESH,
        )

    def ring_arrive(distance):
        for half, way in BOTH:
            ring(half, way, distance).wait_recv()
            for later in (3, 4):
                if later - HOP[later] == distance:
                    send(ring(half, way, later))
        for chunk, entry in enumerate(CHUNKS):
            if entry[2] == distance:
                for half, way in BOTH:
                    send(bulk(half, way, 0, chunk))

    def bulk_arrive(hop, chunk):
        for half, way in BOTH:
            bulk(half, way, hop, chunk).wait_recv()
            if hop < 3:
                send(bulk(half, way, hop + 1, chunk))

    def dense(half, slot):
        across = OFFSETS[slot]
        weight, blocks = [], []
        for other in range(8):
            along = OFFSETS[other]
            if half == 0:
                owner = (x + along + 8) % 8 * 8 + (z + across + 8) % 8
            else:
                owner = (x + across + 8) % 8 * 8 + (z + along + 8) % 8
            weight.append(w_v[:, pl.ds(pl.multiple_of(owner * 128, 128), 128)])
            blocks.append(buf[half, other, slot])
        part = nt(jnp.concatenate(weight, axis=1), jnp.concatenate(blocks, axis=1))
        place = pl.ds(half * 128, 128)
        acc[:, place] = part if slot == 0 else acc[:, place] + part

    def small_copy(stage, k):
        source, target, peer = (
            (small.at[(x + k) % 8], small_1.at[k], along_x(k)),
            (small_2.at[0], small_2.at[k], along_z(k)),
            (small_3.at[0], small_3.at[k], along_x(k)),
        )[stage]
        return pltpu.make_async_remote_copy(
            source, target, small_send.at[stage, k], small_recv.at[stage, k],
            device_id=peer, device_id_type=MESH,
        )

    def small_start():
        for name in ("gy", "ht", "at", "b"):
            loads[name].wait()
        part_gb = exact(nt, b_v[...], gy_v[...])
        part_ha = exact(nn, at_v[...], ht_v[...].reshape(448, 256))
        for piece in range(8):
            group, side = piece // 2, piece % 2
            source = part_gb if group < 2 else part_ha
            small[piece] = source[group % 2 * 8 : group % 2 * 8 + 8, side * 128 : side * 128 + 128]
        for k in FAR_FIRST:
            send(small_copy(0, k))

    def small_second():
        for k in range(1, 8):
            small_copy(0, k).wait_recv()
        total = small[x]
        for k in range(1, 8):
            total = total + small_1[k]
        small_2[0] = total
        for k in range(3, 8):
            opened = (k <= z + 2) | (k >= z + 6)
            pl.when(jnp.logical_not(opened))(lambda k=k: pl.semaphore_wait(ready.at[k], 1))
        for k in FAR_FIRST:
            send(small_copy(1, k))

    def small_third():
        for k in range(1, 8):
            small_copy(1, k).wait_recv()
        total = small_2[0]
        for k in range(1, 8):
            total = total + small_2[k]
        small_3[0] = total
        for k in FAR_FIRST:
            send(small_copy(2, k))

    def small_end():
        small_all[x] = small_3[0]
        for k in range(1, 8):
            small_copy(2, k).wait_recv()
            small_all[(x + 8 - k) % 8] = small_3[k]
        rows = [
            jnp.concatenate([small_all[2 * group], small_all[2 * group + 1]], axis=1)
            for group in range(4)
        ]
        gy_b = jnp.concatenate(rows[:2], axis=0)
        h_a = jnp.concatenate(rows[2:], axis=0)
        grad_a = exact(nt, gy_b, ht_v[...].reshape(448, 256))
        grad_b = exact(nn, h_a, gy_v[...])
        wide = jnp.concatenate([grad_a, jnp.zeros((16, 64), F32), grad_b], axis=1)
        for tile in range(16):
            if tile < 10:
                group, lane = tile // 5, tile % 5 * 128
                value = wide[group * 8 : group * 8 + 8, lane : lane + 128]
            else:
                value = jnp.zeros((8, 128), F32)
            sums[tile // 2, tile % 2, 32:40] = value
        adapter = lax.dot_general(
            at_v[...], gy_b, (((0,), (0,)), ((), ())), precision=HIGHEST,
            preferred_element_type=F32,
        )
        acc[...] += adapter

    def spread_deltas():
        loads["vals"].wait()
        live_slots = count_ref[0]
        side = lax.broadcasted_iota(jnp.int32, (64, 128), 1) // 64
        for k in range(16):
            value = vals_v[k]
            keep = (side == col_ref[k] % 2) & (live_slots > k)
            value = jnp.where(keep, jnp.concatenate([value, value], axis=1), 0.0)
            first, second, _ = pieces(value)
            place = pl.ds(k * 128, 128)
            for block in range(7):
                here = row_ref[k] == block
                rows = pl.ds(block * 64, 64)
                spread[0, rows, place] = jnp.where(here, first, jnp.zeros_like(first))
                spread[1, rows, place] = jnp.where(here, second, jnp.zeros_like(second))

    def choose():
        for k in range(16):
            owner = col_ref[k] // 2
            slot_x = slot_of((owner // 8 - x + 8) % 8)
            slot_z = slot_of((owner % 8 - z + 8) % 8)
            place = pl.ds(k * 128, 128)
            chosen[0:128, place] = buf[0, slot_x, slot_z]
            chosen[128:256, place] = buf[1, slot_z, slot_x]

    def grad_deltas():
        live_slots = count_ref[0]
        lane = lax.broadcasted_iota(jnp.int32, (64, 128), 1)
        for pair in range(8):
            sides = []
            for k in (pair, pair + 8):
                block = nn(ht_v[row_ref[k]], chosen[:, k * 128 : k * 128 + 128])
                block = jnp.where(live_slots > k, block, 0.0)
                swap = (col_ref[k] % 2) != (k // 8)
                sides.append(jnp.where(swap, pltpu.roll(block, 64, 1), block))
            both = jnp.where(lane < 64, sides[0], sides[1])
            sums[pair, 0, 0:32] = both[0:32]
            sums[pair, 1, 0:32] = both[32:64]

    def sums_copy(stage, k):
        source, target, peer = (
            lambda: (sums.at[:, 1 - core], sums_core, other_core),
            lambda: (sums_half.at[(y + k) % 8], sums_y.at[k], along_y(k)),
            lambda: (sums_all.at[y, core], sums_all.at[y, core], along_y(k)),
            lambda: (sums_all.at[(y + 8 - k) % 8, core], sums_all.at[(y + 8 - k) % 8, core], other_core),
        )[stage]()
        return pltpu.make_async_remote_copy(
            source, target, sums_send.at[stage, k], sums_recv.at[stage, k],
            device_id=peer, device_id_type=MESH,
        )

    for way in (0, 1):
        send(ring(0, way, 1))
    for way in (0, 1):
        send(bulk(1, way, 0, 0))
    for way in (0, 1):
        send(ring(0, way, 2))
    to_z = {
        1: [ring(1, 0, 1), bulk(0, 0, 0, 0)],
        2: [ring(1, 0, 2)],
        -1: [ring(1, 1, 1), bulk(0, 1, 0, 0)],
        -2: [ring(1, 1, 2)],
    }

    def open_z(offset, wait):
        if wait:
            pl.semaphore_wait(ready.at[(z + offset + 8) % 8], 1)
        for copy in to_z[offset]:
            copy.start()

    for copies in to_z.values():
        sent.extend(copies)
    pl.when(z >= 1)(lambda: open_z(-1, False))
    pl.when(z >= 2)(lambda: open_z(-2, False))
    pl.when(z >= 7)(lambda: open_z(1, False))
    pl.when(z >= 6)(lambda: open_z(2, False))
    small_start()
    pl.when(z < 7)(lambda: open_z(1, True))
    pl.when(z < 6)(lambda: open_z(2, True))
    pl.when(z < 2)(lambda: open_z(-2, True))
    pl.when(z < 1)(lambda: open_z(-1, True))

    ring_arrive(1)
    ring_arrive(2)
    bulk_arrive(0, 0)

    ring_arrive(3)
    ring_arrive(4)
    bulk_arrive(1, 0)
    bulk_arrive(0, 1)
    bulk_arrive(0, 2)
    small_second()
    loads["w"].wait()
    dense(0, 0)
    dense(1, 0)

    for wave in range(2, 6):
        for chunk in range(5):
            hop = wave - (0, 1, 1, 2, 2)[chunk]
            if hop < 4:
                bulk_arrive(hop, chunk)
        if wave == 2:
            spread_deltas()
        if wave == 3:
            small_third()
        hop = wave - 2
        if hop < 3:
            for half, way in BOTH:
                dense(half, ring_slot(STEP[way], hop + 1))
        if wave == 4:
            small_end()

    choose()
    grad_deltas()
    pl.when(core == 0)(lambda: pl.semaphore_wait(ready_core, 1))
    send(sums_copy(0, 0))
    sums_copy(0, 0).wait_recv()
    sums_half[...] = sums[:, core] + sums_core[...]
    for k in FAR_FIRST:
        send(sums_copy(1, k))
    dense(0, 7)
    dense(1, 7)
    total = acc[...]
    for part in (1, 0):
        total = total + nt(spread[part], chosen[...])
    gh_v[...] = total.astype(BF16)
    gh_copy = pltpu.make_async_copy(gh_v, gh_out, load_sem.at[0])
    gh_copy.start()
    total = sums_half[y]
    for k in range(1, 8):
        sums_copy(1, k).wait_recv()
        total = total + sums_y[k]
    sums_all[y, core] = total
    for k in FAR_FIRST:
        send(sums_copy(2, k))
    send(sums_copy(3, 0))
    for k in FAR_FIRST[::-1]:
        sums_copy(2, k).wait_recv()
        send(sums_copy(3, k))
    for k in range(8):
        sums_copy(3, k).wait_recv()
    sums_write = pltpu.make_async_copy(sums_all, sums_out, load_sem.at[1])
    sums_write.start()
    for copy in sent:
        copy.wait_send()
    gh_copy.wait()
    sums_write.wait()


def finish(gh_in, sums_in, gh_out, ga_out, gb_out, gd_out):
    gh_out[...] = gh_in[...]
    for pair in range(8):
        for side in (0, 1):
            value = sums_in[pair, side]
            rows = pl.ds(side * 32, 32)
            gd_out[pair, rows] = value[0:32, 0:64]
            gd_out[pair + 8, rows] = value[0:32, 64:128]
            tile = 2 * pair + side
            if tile < 10:
                group, lane = pl.ds(tile // 5 * 8, 8), tile % 5
                if lane < 3:
                    ga_out[group, lane * 128 : lane * 128 + 128] = value[32:40]
                elif lane == 3:
                    ga_out[group, 384:448] = value[32:40, 0:64]
                else:
                    gb_out[group, :] = value[32:40]


def on_device(
    grad_out, hidden, base_weight, adapt_a, adapt_b, delta_vals, blk_row, blk_col, blk_count
):
    hbm = pl.BlockSpec(memory_space=pltpu.HBM)
    scalar = pl.BlockSpec(memory_space=pltpu.SMEM)
    vmem = pl.BlockSpec(memory_space=pltpu.VMEM)
    dma = pltpu.SemaphoreType.DMA
    small_tiles = pltpu.VMEM((8, 8, 128), F32)
    gathered, summed = pl.pallas_call(
        kernel,
        out_shape=(
            jax.ShapeDtypeStruct((448, 256), BF16),
            jax.ShapeDtypeStruct((8, 2, 40, 128), F32),
        ),
        in_specs=[hbm] * 6 + [scalar] * 3,
        out_specs=(hbm, hbm),
        scratch_shapes=[
            pltpu.VMEM((2, 8, 8, 128, 128), BF16),
            pltpu.VMEM((256, 128), BF16),
            pltpu.VMEM((7, 64, 256), BF16),
            pltpu.VMEM((448, 8192), BF16),
            pltpu.VMEM((16, 448), F32),
            pltpu.VMEM((16, 128), F32),
            pltpu.VMEM((16, 64, 64), F32),
            dma((8,)),
            pltpu.VMEM((448, 256), F32),
            pltpu.VMEM((2, 448, 2048), BF16),
            pltpu.VMEM((256, 2048), BF16),
            pltpu.VMEM((448, 256), BF16),
            dma((2, 2, 4)),
            dma((2, 2, 4)),
            dma((2, 2, 4, 5)),
            dma((2, 2, 4, 5)),
            pltpu.SemaphoreType.REGULAR((8,)),
            pltpu.SemaphoreType.REGULAR,
            small_tiles,
            small_tiles,
            small_tiles,
            small_tiles,
            small_tiles,
            dma((3, 8)),
            dma((3, 8)),
            pltpu.VMEM((8, 2, 40, 128), F32),
            pltpu.VMEM((8, 40, 128), F32),
            pltpu.VMEM((8, 40, 128), F32),
            pltpu.VMEM((8, 40, 128), F32),
            pltpu.VMEM((8, 2, 40, 128), F32),
            dma((4, 8)),
            dma((4, 8)),
        ],
        compiler_params=pltpu.CompilerParams(
            collective_id=0, has_side_effects=True, vmem_limit_bytes=60 << 20
        ),
        cost_estimate=pl.CostEstimate(
            flops=3_000_000_000, bytes_accessed=12_000_000, transcendentals=0
        ),
    )(
        grad_out, hidden.T.reshape(7, 64, 256), base_weight, adapt_a.T, adapt_b, delta_vals,
        blk_row, blk_col, blk_count,
    )
    gh, ga, gb, gd = pl.pallas_call(
        finish,
        out_shape=(
            jax.ShapeDtypeStruct((448, 256), BF16),
            jax.ShapeDtypeStruct((16, 448), F32),
            jax.ShapeDtypeStruct((16, 128), F32),
            jax.ShapeDtypeStruct((16, 64, 64), F32),
        ),
        in_specs=[vmem] * 2,
        out_specs=(vmem,) * 4,
        compiler_params=pltpu.CompilerParams(vmem_limit_bytes=60 << 20),
    )(gathered, summed)
    return gh.T, ga.T, gb, gd


def solution(mesh):
    placed = (
        P("dp", "fsdp"),
        P("dp", "fsdp"),
        P("fsdp", None),
        P("fsdp", None),
        P(None, "fsdp"),
        P("fsdp", None, None),
        P("fsdp"),
        P("fsdp"),
        P("fsdp"),
    )
    return jax.shard_map(
        on_device,
        mesh=mesh,
        in_specs=placed,
        out_specs=(P("dp", "fsdp"), P("fsdp", None), P(None, "fsdp"), P("fsdp", None, None)),
        check_vma=False,
    )
```

```python
import jax
import jax.numpy as jnp
from jax import lax
from jax.experimental import pallas as pl
from jax.experimental.pallas import tpu as pltpu
from jax.sharding import PartitionSpec as P

MESH = pl.DeviceIdType.MESH
BF16, F32 = jnp.bfloat16, jnp.float32
HIGHEST = lax.Precision.HIGHEST
OFFSETS = (0, 1, -1, 2, -2, 3, -3, 4)
CHUNKS = ((0, 1, 0), (1, 2, 1), (3, 2, 2), (5, 2, 3), (7, 1, 4))
BOTH = tuple((half, way) for way in (0, 1) for half in (0, 1))
STEP = (1, -1)
FAR_FIRST = (4, 3, 5, 2, 6, 1, 7)
HOP = {1: 1, 2: 2, 3: 1, 4: 2}


def ring_slot(step, distance):
    if distance in (0, 4):
        return 0 if distance == 0 else 7
    return 2 * distance - 1 if step == -1 else 2 * distance


def slot_of(offset):
    return jnp.where(offset == 0, 0, jnp.where(offset <= 4, 2 * offset - 1, 16 - 2 * offset))


def nt(a, b):
    return lax.dot_general(a, b, (((1,), (1,)), ((), ())), preferred_element_type=F32)


def nn(a, b):
    return lax.dot_general(a, b, (((1,), (0,)), ((), ())), preferred_element_type=F32)


def pieces(value):
    first = value.astype(BF16)
    rest = value - first.astype(F32)
    second = rest.astype(BF16)
    third = (rest - second.astype(F32)).astype(BF16)
    return first, second, third


def exact(product, value, other):
    return sum(product(piece, other) for piece in pieces(value)[::-1])


def kernel(
    gy_hbm, ht_hbm, w_hbm, at_hbm, b_hbm, vals_hbm, row_ref, col_ref, count_ref,
    gh_out, sums_out,
    buf, gy_v, ht_v, w_v, at_v, b_v, vals_v, load_sem,
    acc, spread, chosen, gh_v,
    ring_send, ring_recv, bulk_send, bulk_recv,
    small, small_1, small_2, small_3, small_all, small_send, small_recv,
    sums, sums_core, sums_half, sums_y, sums_all, sums_send, sums_recv,
):
    f = lax.axis_index("fsdp")
    d = lax.axis_index("dp")
    x, z, y, core = f // 8, f % 8, d // 2, d % 2

    def along_x(k):
        return ((x + k + 8) % 8 * 8 + z, d)

    def along_z(k):
        return (x * 8 + (z + k + 8) % 8, d)

    def along_y(k):
        return (f, (y + k + 8) % 8 * 2 + core)

    other_core = (f, y * 2 + 1 - core)

    def first_axis(half, k):
        return along_z(k) if half else along_x(k)

    def second_axis(half, k):
        return along_x(k) if half else along_z(k)

    barrier = pltpu.get_barrier_semaphore()
    peers = [way(k) for way in (along_x, along_z, along_y) for k in range(1, 8)] + [other_core]
    for peer in peers:
        pl.semaphore_signal(barrier, inc=1, device_id=peer, device_id_type=MESH)

    loads = {
        "gy0": pltpu.make_async_copy(gy_hbm.at[pl.ds(0, 128)], buf.at[0, 0, 0], load_sem.at[0]),
        "gy1": pltpu.make_async_copy(gy_hbm.at[pl.ds(128, 128)], buf.at[1, 0, 0], load_sem.at[1]),
        "gy": pltpu.make_async_copy(gy_hbm, gy_v, load_sem.at[2]),
        "ht": pltpu.make_async_copy(ht_hbm, ht_v, load_sem.at[3]),
        "at": pltpu.make_async_copy(at_hbm, at_v, load_sem.at[4]),
        "b": pltpu.make_async_copy(b_hbm, b_v, load_sem.at[5]),
        "vals": pltpu.make_async_copy(vals_hbm, vals_v, load_sem.at[6]),
        "w": pltpu.make_async_copy(w_hbm, w_v, load_sem.at[7]),
    }
    for load in loads.values():
        load.start()
    loads["gy0"].wait()
    loads["gy1"].wait()
    pl.semaphore_wait(barrier, len(peers))

    sent = []

    def send(copy):
        copy.start()
        sent.append(copy)

    def ring(half, way, distance):
        step = STEP[way]
        source, target = ring_slot(step, distance - HOP[distance]), ring_slot(step, distance)
        rows = pl.ds(0, 128) if distance < 4 else pl.ds(way * 64, 64)
        return pltpu.make_async_remote_copy(
            buf.at[half, source, 0, rows], buf.at[half, target, 0, rows],
            ring_send.at[half, way, distance - 1], ring_recv.at[half, way, distance - 1],
            device_id=first_axis(half, step * HOP[distance]), device_id_type=MESH,
        )

    def bulk(half, way, hop, chunk):
        step = STEP[way]
        source, target = ring_slot(step, hop), ring_slot(step, hop + 1)
        rows = pl.ds(0, 128) if hop < 3 else pl.ds(way * 64, 64)
        slots = pl.ds(CHUNKS[chunk][0], CHUNKS[chunk][1])
        return pltpu.make_async_remote_copy(
            buf.at[half, slots, source, rows], buf.at[half, slots, target, rows],
            bulk_send.at[half, way, hop, chunk], bulk_recv.at[half, way, hop, chunk],
            device_id=second_axis(half, step), device_id_type=MESH,
        )

    def ring_arrive(distance):
        for half, way in BOTH:
            ring(half, way, distance).wait_recv()
            for later in (3, 4):
                if later - HOP[later] == distance:
                    send(ring(half, way, later))
        for chunk, entry in enumerate(CHUNKS):
            if entry[2] == distance:
                for half, way in BOTH:
                    send(bulk(half, way, 0, chunk))

    def bulk_arrive(hop, chunk):
        for half, way in BOTH:
            bulk(half, way, hop, chunk).wait_recv()
            if hop < 3:
                send(bulk(half, way, hop + 1, chunk))

    def dense(half, slot):
        across = OFFSETS[slot]
        weight, blocks = [], []
        for other in range(8):
            along = OFFSETS[other]
            if half == 0:
                owner = (x + along + 8) % 8 * 8 + (z + across + 8) % 8
            else:
                owner = (x + across + 8) % 8 * 8 + (z + along + 8) % 8
            weight.append(w_v[:, pl.ds(pl.multiple_of(owner * 128, 128), 128)])
            blocks.append(buf[half, other, slot])
        part = nt(jnp.concatenate(weight, axis=1), jnp.concatenate(blocks, axis=1))
        place = pl.ds(half * 128, 128)
        acc[:, place] = part if slot == 0 else acc[:, place] + part

    def small_copy(stage, k):
        source, target, peer = (
            (small.at[(x + k) % 8], small_1.at[k], along_x(k)),
            (small_2.at[0], small_2.at[k], along_z(k)),
            (small_3.at[0], small_3.at[k], along_x(k)),
        )[stage]
        return pltpu.make_async_remote_copy(
            source, target, small_send.at[stage, k], small_recv.at[stage, k],
            device_id=peer, device_id_type=MESH,
        )

    def small_start():
        for name in ("gy", "ht", "at", "b"):
            loads[name].wait()
        part_gb = exact(nt, b_v[...], gy_v[...])
        part_ha = exact(nn, at_v[...], ht_v[...].reshape(448, 256))
        for piece in range(8):
            group, side = piece // 2, piece % 2
            source = part_gb if group < 2 else part_ha
            small[piece] = source[group % 2 * 8 : group % 2 * 8 + 8, side * 128 : side * 128 + 128]
        for k in range(1, 8):
            send(small_copy(0, k))

    def small_second():
        for k in range(1, 8):
            small_copy(0, k).wait_recv()
        total = small[x]
        for k in range(1, 8):
            total = total + small_1[k]
        small_2[0] = total
        for k in range(1, 8):
            send(small_copy(1, k))

    def small_third():
        for k in range(1, 8):
            small_copy(1, k).wait_recv()
        total = small_2[0]
        for k in range(1, 8):
            total = total + small_2[k]
        small_3[0] = total
        for k in range(1, 8):
            send(small_copy(2, k))

    def small_end():
        small_all[x] = small_3[0]
        for k in range(1, 8):
            small_copy(2, k).wait_recv()
            small_all[(x + 8 - k) % 8] = small_3[k]
        rows = [
            jnp.concatenate([small_all[2 * group], small_all[2 * group + 1]], axis=1)
            for group in range(4)
        ]
        gy_b = jnp.concatenate(rows[:2], axis=0)
        h_a = jnp.concatenate(rows[2:], axis=0)
        grad_a = exact(nt, gy_b, ht_v[...].reshape(448, 256))
        grad_b = exact(nn, h_a, gy_v[...])
        wide = jnp.concatenate([grad_a, jnp.zeros((16, 64), F32), grad_b], axis=1)
        for tile in range(16):
            if tile < 10:
                group, lane = tile // 5, tile % 5 * 128
                value = wide[group * 8 : group * 8 + 8, lane : lane + 128]
            else:
                value = jnp.zeros((8, 128), F32)
            sums[tile // 2, tile % 2, 32:40] = value
        adapter = lax.dot_general(
            at_v[...], gy_b, (((0,), (0,)), ((), ())), precision=HIGHEST,
            preferred_element_type=F32,
        )
        acc[...] += adapter

    def spread_deltas():
        loads["vals"].wait()
        live_slots = count_ref[0]
        side = lax.broadcasted_iota(jnp.int32, (64, 128), 1) // 64
        for k in range(16):
            value = vals_v[k]
            keep = (side == col_ref[k] % 2) & (live_slots > k)
            value = jnp.where(keep, jnp.concatenate([value, value], axis=1), 0.0)
            first, second, _ = pieces(value)
            place = pl.ds(k * 128, 128)
            for block in range(7):
                here = row_ref[k] == block
                rows = pl.ds(block * 64, 64)
                spread[0, rows, place] = jnp.where(here, first, jnp.zeros_like(first))
                spread[1, rows, place] = jnp.where(here, second, jnp.zeros_like(second))

    def choose():
        for k in range(16):
            owner = col_ref[k] // 2
            slot_x = slot_of((owner // 8 - x + 8) % 8)
            slot_z = slot_of((owner % 8 - z + 8) % 8)
            place = pl.ds(k * 128, 128)
            chosen[0:128, place] = buf[0, slot_x, slot_z]
            chosen[128:256, place] = buf[1, slot_z, slot_x]

    def grad_deltas():
        live_slots = count_ref[0]
        lane = lax.broadcasted_iota(jnp.int32, (64, 128), 1)
        for pair in range(8):
            sides = []
            for k in (pair, pair + 8):
                block = nn(ht_v[row_ref[k]], chosen[:, k * 128 : k * 128 + 128])
                block = jnp.where(live_slots > k, block, 0.0)
                swap = (col_ref[k] % 2) != (k // 8)
                sides.append(jnp.where(swap, pltpu.roll(block, 64, 1), block))
            both = jnp.where(lane < 64, sides[0], sides[1])
            sums[pair, 0, 0:32] = both[0:32]
            sums[pair, 1, 0:32] = both[32:64]

    def sums_copy(stage, k):
        source, target, peer = (
            lambda: (sums.at[:, 1 - core], sums_core, other_core),
            lambda: (sums_half.at[(y + k) % 8], sums_y.at[k], along_y(k)),
            lambda: (sums_all.at[y, core], sums_all.at[y, core], along_y(k)),
            lambda: (sums_all.at[(y + 8 - k) % 8, core], sums_all.at[(y + 8 - k) % 8, core], other_core),
        )[stage]()
        return pltpu.make_async_remote_copy(
            source, target, sums_send.at[stage, k], sums_recv.at[stage, k],
            device_id=peer, device_id_type=MESH,
        )

    for half, way in BOTH:
        send(ring(half, way, 1))
    for half, way in BOTH:
        send(bulk(half, way, 0, 0))
    for half, way in BOTH:
        send(ring(half, way, 2))
    small_start()

    ring_arrive(1)
    ring_arrive(2)
    bulk_arrive(0, 0)

    ring_arrive(3)
    ring_arrive(4)
    bulk_arrive(1, 0)
    bulk_arrive(0, 1)
    bulk_arrive(0, 2)
    small_second()
    loads["w"].wait()
    dense(0, 0)
    dense(1, 0)

    for wave in range(2, 6):
        for chunk in range(5):
            hop = wave - (0, 1, 1, 2, 2)[chunk]
            if hop < 4:
                bulk_arrive(hop, chunk)
        if wave == 2:
            spread_deltas()
        if wave == 3:
            small_third()
        hop = wave - 2
        if hop < 3:
            for half, way in BOTH:
                dense(half, ring_slot(STEP[way], hop + 1))
        if wave == 4:
            small_end()

    choose()
    grad_deltas()
    send(sums_copy(0, 0))
    sums_copy(0, 0).wait_recv()
    sums_half[...] = sums[:, core] + sums_core[...]
    for k in FAR_FIRST:
        send(sums_copy(1, k))
    dense(0, 7)
    dense(1, 7)
    total = acc[...]
    for part in (1, 0):
        total = total + nt(spread[part], chosen[...])
    gh_v[...] = total.astype(BF16)
    gh_copy = pltpu.make_async_copy(gh_v, gh_out, load_sem.at[0])
    gh_copy.start()
    total = sums_half[y]
    for k in range(1, 8):
        sums_copy(1, k).wait_recv()
        total = total + sums_y[k]
    sums_all[y, core] = total
    for k in FAR_FIRST:
        send(sums_copy(2, k))
    send(sums_copy(3, 0))
    for k in FAR_FIRST[::-1]:
        sums_copy(2, k).wait_recv()
        send(sums_copy(3, k))
    for k in range(8):
        sums_copy(3, k).wait_recv()
    sums_write = pltpu.make_async_copy(sums_all, sums_out, load_sem.at[1])
    sums_write.start()
    for copy in sent:
        copy.wait_send()
    gh_copy.wait()
    sums_write.wait()


def finish(gh_in, sums_in, gh_out, ga_out, gb_out, gd_out):
    gh_out[...] = gh_in[...]
    for pair in range(8):
        for side in (0, 1):
            value = sums_in[pair, side]
            rows = pl.ds(side * 32, 32)
            gd_out[pair, rows] = value[0:32, 0:64]
            gd_out[pair + 8, rows] = value[0:32, 64:128]
            tile = 2 * pair + side
            if tile < 10:
                group, lane = pl.ds(tile // 5 * 8, 8), tile % 5
                if lane < 3:
                    ga_out[group, lane * 128 : lane * 128 + 128] = value[32:40]
                elif lane == 3:
                    ga_out[group, 384:448] = value[32:40, 0:64]
                else:
                    gb_out[group, :] = value[32:40]


def on_device(
    grad_out, hidden, base_weight, adapt_a, adapt_b, delta_vals, blk_row, blk_col, blk_count
):
    hbm = pl.BlockSpec(memory_space=pltpu.HBM)
    scalar = pl.BlockSpec(memory_space=pltpu.SMEM)
    vmem = pl.BlockSpec(memory_space=pltpu.VMEM)
    dma = pltpu.SemaphoreType.DMA
    small_tiles = pltpu.VMEM((8, 8, 128), F32)
    gathered, summed = pl.pallas_call(
        kernel,
        out_shape=(
            jax.ShapeDtypeStruct((448, 256), BF16),
            jax.ShapeDtypeStruct((8, 2, 40, 128), F32),
        ),
        in_specs=[hbm] * 6 + [scalar] * 3,
        out_specs=(hbm, hbm),
        scratch_shapes=[
            pltpu.VMEM((2, 8, 8, 128, 128), BF16),
            pltpu.VMEM((256, 128), BF16),
            pltpu.VMEM((7, 64, 256), BF16),
            pltpu.VMEM((448, 8192), BF16),
            pltpu.VMEM((16, 448), F32),
            pltpu.VMEM((16, 128), F32),
            pltpu.VMEM((16, 64, 64), F32),
            dma((8,)),
            pltpu.VMEM((448, 256), F32),
            pltpu.VMEM((2, 448, 2048), BF16),
            pltpu.VMEM((256, 2048), BF16),
            pltpu.VMEM((448, 256), BF16),
            dma((2, 2, 4)),
            dma((2, 2, 4)),
            dma((2, 2, 4, 5)),
            dma((2, 2, 4, 5)),
            small_tiles,
            small_tiles,
            small_tiles,
            small_tiles,
            small_tiles,
            dma((3, 8)),
            dma((3, 8)),
            pltpu.VMEM((8, 2, 40, 128), F32),
            pltpu.VMEM((8, 40, 128), F32),
            pltpu.VMEM((8, 40, 128), F32),
            pltpu.VMEM((8, 40, 128), F32),
            pltpu.VMEM((8, 2, 40, 128), F32),
            dma((4, 8)),
            dma((4, 8)),
        ],
        compiler_params=pltpu.CompilerParams(
            collective_id=0, has_side_effects=True, vmem_limit_bytes=60 << 20
        ),
        cost_estimate=pl.CostEstimate(
            flops=3_000_000_000, bytes_accessed=12_000_000, transcendentals=0
        ),
    )(
        grad_out, hidden.T.reshape(7, 64, 256), base_weight, adapt_a.T, adapt_b, delta_vals,
        blk_row, blk_col, blk_count,
    )
    gh, ga, gb, gd = pl.pallas_call(
        finish,
        out_shape=(
            jax.ShapeDtypeStruct((448, 256), BF16),
            jax.ShapeDtypeStruct((16, 448), F32),
            jax.ShapeDtypeStruct((16, 128), F32),
            jax.ShapeDtypeStruct((16, 64, 64), F32),
        ),
        in_specs=[vmem] * 2,
        out_specs=(vmem,) * 4,
        compiler_params=pltpu.CompilerParams(vmem_limit_bytes=60 << 20),
    )(gathered, summed)
    return gh.T, ga.T, gb, gd


def solution(mesh):
    placed = (
        P("dp", "fsdp"),
        P("dp", "fsdp"),
        P("fsdp", None),
        P("fsdp", None),
        P(None, "fsdp"),
        P("fsdp", None, None),
        P("fsdp"),
        P("fsdp"),
        P("fsdp"),
    )
    return jax.shard_map(
        on_device,
        mesh=mesh,
        in_specs=placed,
        out_specs=(P("dp", "fsdp"), P("fsdp", None), P(None, "fsdp"), P("fsdp", None, None)),
        check_vma=False,
    )
```
